32 devices in a mesh: dp: 1, expert: 32 (over z, y, x, core).
Axes of the slice: x: 2, y: 2, z: 4, core: 2. Of those that a mesh axis runs over, the one named last changes fastest.
Arguments:
- tokens: bfloat16 [4096, 2048], P(('dp', 'expert')), may hold values from -6 to 6
- upstream: bfloat16 [4096, 2048], P(('dp', 'expert')), may hold values from -6 to 6
- w_up: bfloat16 [32, 2048, 768], P('expert'), may hold values from -0.125 to 0.125
- w_down: bfloat16 [32, 2048, 768], P('expert'), may hold values from -0.21875 to 0.21875
- routes: int32 [4096, 1], P(('dp', 'expert')), may hold values from 0 to 31; in each aligned block of 128 rows (0 to 127, 128 to 255, ...) at most 6 rows name the same one
- gate_share: int32 [4096, 1], P(('dp', 'expert')), may hold values from 1 to 256
Outputs:
- token_grad: bfloat16 [4096, 2048], P(('dp', 'expert'))
- gate_grad: bfloat16 [4096, 1], P(('dp', 'expert'))
- up_grad: float32 [32, 2048, 768], P('expert', 'dp')
- down_grad: float32 [32, 2048, 768], P('expert', 'dp')
The draws below stay inside these ranges and needn't reach their ends.
Inputs may be any that keep to these rules, and one draw needn't show every extreme that they name: `routes`: within the 128 tokens of one device each expert is named by at most 6 rows, and by exactly 6 for some expert.
All inputs are finite; a program needn't handle non-finite values.
Results may differ from the reference program's by a relative error of at most 0.013.
Values may be sent and summed in bfloat16 or wider, within the bound.
A program may use at most 64 MiB of HBM per device.

```python
import math
import jax
import jax.numpy as jnp
import numpy as np
from jax import lax

D = 2048
F = 768
TOPK = 1
GATE_DEN = 256
TOK_DEV = 128
EXPERTS = 32
CAP = 6
TOKENS = 4096
N_DP = 1
N_EXPERT = 32


def touch_ends(entries, stream_key, smallest, high):
    dims = entries.shape
    place = [jax.random.randint(jax.random.fold_in(stream_key, axis), (), 0, dims[axis]) for axis in range(len(dims))]
    entries = entries.at[tuple(place)].set(smallest)
    longest = dims.index(max(dims))
    place[longest] = (place[longest] + 1) % dims[longest]
    return entries.at[tuple(place)].set(high)


def strengthened(result, own_key, source, target, shards_of, factor):
    owner, partner = [(jnp.arange(result.shape[position]) // (result.shape[position] // shards_of)).reshape([-1 if axis == position else 1 for axis in range(result.ndim)]) for position in (source, target)]
    chosen = jax.random.permutation(own_key, shards_of)[partner]
    strong = (owner == chosen) | (owner == (partner + shards_of // 2) % shards_of)
    return jnp.where(strong, factor * result, result)


def steps_of(stream_key, dims, cuts, smallest, high):
    def one(dim, blocks):
        draws = jax.random.uniform(jax.random.fold_in(jax.random.fold_in(stream_key, 6), dim), (blocks,), jnp.float32, smallest / len(cuts), high / len(cuts))
        return jnp.repeat(jnp.exp(draws), dims[dim] // blocks).reshape((-1,) + (1,) * (len(dims) - dim - 1))

    factor_of = one(*cuts[0])
    for cut in cuts[1:]:
        factor_of = factor_of * one(*cut)
    return factor_of


def routed_block(rng, own, number, rows, amount, top, most, skew):
    ranking = jax.random.permutation(rng, amount)
    heavy_load, common = shares(amount, rows * top, most, skew, True), shares(amount, rows * top, most, skew, False)
    places = jnp.arange(amount)

    def named(tallies, offset_by):
        used = int((tallies > 0).sum())
        fixed = max(1, used // 4)
        moved = fixed + (places - fixed + offset_by * (used - fixed)) % max(1, amount - fixed)
        return jnp.zeros((amount,), jnp.int32).at[ranking[jnp.where(places < fixed, places, moved)]].set(jnp.asarray(tallies, jnp.int32))

    tallies = jnp.where(number % 4 == 0, named(heavy_load, number // 4), named(common, number - number // 4 - 1))
    mixed = jax.random.permutation(jax.random.fold_in(own, 3), amount)
    giver, taker = mixed[0:amount // 2 * 2:2], mixed[1:amount // 2 * 2:2]
    slack = jnp.minimum(tallies[giver] - 1, most - tallies[taker]) // 2
    slack = jnp.where((giver == ranking[0]) | (taker == ranking[0]) | (tallies[taker] == 0), 0, jnp.maximum(slack, 0))
    moved = jax.random.randint(jax.random.fold_in(own, 4), (amount // 2,), 0, 1 << 20) % (slack + 1)
    tallies = tallies.at[giver].add(-moved).at[taker].add(moved)
    members = jnp.searchsorted(jnp.cumsum(tallies), jnp.arange(rows * top), side="right").astype(jnp.int32)
    grid = members.reshape(top, rows).T
    grid = grid[jax.random.permutation(jax.random.fold_in(own, 1), rows)]
    offset_by = jax.random.randint(jax.random.fold_in(own, 2), (rows, 1), 0, top)
    return jnp.take_along_axis(grid, (jnp.arange(top)[None, :] + offset_by) % top, axis=1)


def shares(count, total, reach, lean, full):
    weights = [(1 << 20) // math.isqrt(standing ** lean) + 1 for standing in range(1, count + 1)]
    largest = reach if full else min(reach, max(-(-total // count), total * weights[0] // sum(weights)))
    least = 1 if total - largest >= count - 1 else 0
    counts, surplus = [largest] + [least] * (count - 1), total - largest - least * (count - 1)
    while surplus > 0:
        candidates = [i for i in range(1, count) if counts[i] < largest] or [i for i in range(1, count) if counts[i] < reach]
        whole, budget = sum([weights[i] for i in candidates]), surplus
        for i in candidates:
            addition = min(reach - counts[i], max(1, budget * weights[i] // whole), surplus)
            counts[i] = counts[i] + addition
            surplus = surplus - addition
    return np.array(counts)


def noise(key, shape, spread, bound, cuts=(), kind=jnp.bfloat16):
    drawn = spread * jax.random.normal(key, shape, jnp.float32)
    if cuts:
        drawn = drawn * steps_of(key, shape, cuts, -0.22, 0.18)
    return jnp.clip(drawn, -bound, bound).astype(kind)


def heavy_noise(stream_key, extent, spread, reach, pieces, heavy, kind=jnp.bfloat16):
    array = spread * jax.random.normal(stream_key, extent, jnp.float32)
    if pieces:
        array = array * steps_of(stream_key, extent, pieces, -0.22, 0.18)
    return jnp.clip(strengthened(array, jax.random.fold_in(stream_key, 3), *heavy), -reach, reach).astype(kind)


def setup_inputs(seed: int = 0) -> dict:
    keys = jax.random.split(jax.random.key(seed), 7)
    tokens = heavy_noise(keys[0], (TOKENS, D), 1.0, 6.0, ((0, 32),), (0, 1, 32, 2.75))
    upstream = noise(keys[1], (TOKENS, D), 1.0, 6.0, ((0, 32),))
    w_up = noise(keys[2], (EXPERTS, D, F), D ** -0.5, 0.125, ((0, 32),))
    w_down = noise(keys[3], (EXPERTS, D, F), F ** -0.5, 0.21875, ((0, 32),))
    routes_keys = jax.random.split(jax.random.fold_in(keys[4], 1), TOKENS // TOK_DEV)
    routes_turns = jax.random.permutation(jax.random.fold_in(keys[4], 3), TOKENS // TOK_DEV)
    routes = jax.vmap(lambda own, number: routed_block(jax.random.fold_in(keys[4], 2), own, number, TOK_DEV, EXPERTS, TOPK, CAP, 2))(routes_keys, routes_turns).reshape((TOKENS, TOPK))
    gate_share = touch_ends(jax.random.randint(keys[5], (TOKENS, TOPK), 1, GATE_DEN + 1), jax.random.fold_in(keys[5], 1), 1, GATE_DEN).astype(jnp.int32)
    return {"tokens": tokens, "upstream": upstream, "w_up": w_up, "w_down": w_down, "routes": routes, "gate_share": gate_share}


def reference(tokens, upstream, w_up, w_down, routes, gate_share):
    token_total = tokens.shape[0]
    top_count = routes.shape[1]
    expert_total = w_up.shape[0]
    flat_routes = routes.reshape(-1).astype(jnp.int32)
    row_total = flat_routes.shape[0]
    row_ids = jnp.arange(row_total, dtype=jnp.int32)
    device_id = row_ids // (TOK_DEV * top_count)
    keyed = device_id * expert_total + flat_routes
    sort_order = jnp.argsort(keyed, stable=True).astype(jnp.int32)
    sorted_keys = keyed[sort_order]
    run_start = jnp.searchsorted(sorted_keys, sorted_keys, side="left").astype(jnp.int32)
    rank_sorted = (row_ids - run_start).astype(jnp.int32)
    slot_rank = jnp.zeros((row_total,), jnp.int32).at[sort_order].set(rank_sorted)
    data_group = device_id // N_EXPERT
    source_id = device_id % N_EXPERT
    slot_table = jnp.full((expert_total, N_DP, N_EXPERT * CAP), row_total, jnp.int32)
    slot_table = slot_table.at[flat_routes, data_group, source_id * CAP + slot_rank].set(row_ids)
    gate_values = gate_share.reshape(-1).astype(jnp.float32) / GATE_DEN

    def one_expert(carry, operands):
        grad_rows, gate_rows = carry
        slots, up_weight, down_weight = operands
        in_use = slots < row_total
        safe_rows = jnp.where(in_use, slots, 0)
        token_ids = safe_rows // top_count
        mask = in_use[..., None]
        inputs = jnp.where(mask, tokens[token_ids].astype(jnp.float32), 0.0)
        cotan = jnp.where(mask, upstream[token_ids].astype(jnp.float32), 0.0)
        gates = jnp.where(in_use, gate_values[safe_rows], 0.0)
        up_f = up_weight.astype(jnp.float32)
        down_f = down_weight.astype(jnp.float32)
        pre_act = jnp.einsum("gsd,df->gsf", inputs, up_f)
        hidden = jax.nn.silu(pre_act).astype(jnp.bfloat16)
        expert_out = jnp.einsum("gsf,df->gsd", hidden.astype(jnp.float32), down_f)
        gate_grad = jnp.sum(expert_out * cotan, axis=-1).astype(jnp.bfloat16)
        scaled = (gates[..., None] * cotan).astype(jnp.bfloat16)
        hidden_grad = jnp.einsum("gsd,df->gsf", scaled.astype(jnp.float32), down_f)
        sigmoid_a = jax.nn.sigmoid(pre_act)
        pre_grad = (hidden_grad * sigmoid_a * (1.0 + pre_act * (1.0 - sigmoid_a))).astype(jnp.bfloat16)
        row_grad = jnp.einsum("gsf,df->gsd", pre_grad.astype(jnp.float32), up_f).astype(jnp.bfloat16)
        part_up = jnp.einsum("gsd,gsf->gdf", inputs, pre_grad.astype(jnp.float32)).astype(jnp.bfloat16)
        part_up = lax.optimization_barrier(part_up)
        part_down = jnp.einsum("gsd,gsf->gdf", scaled.astype(jnp.float32), hidden.astype(jnp.float32)).astype(jnp.bfloat16)
        part_down = lax.optimization_barrier(part_down)
        up_sum = jnp.sum(part_up.astype(jnp.float32), axis=0)
        down_sum = jnp.sum(part_down.astype(jnp.float32), axis=0)
        flat_slots = slots.reshape(-1)
        grad_rows = grad_rows.at[flat_slots].set(row_grad.reshape(-1, row_grad.shape[-1]).astype(jnp.float32), mode="drop")
        gate_rows = gate_rows.at[flat_slots].set(gate_grad.reshape(-1).astype(jnp.float32), mode="drop")
        return (grad_rows, gate_rows), (up_sum, down_sum)

    start_rows = jnp.zeros((row_total, tokens.shape[1]), jnp.float32)
    start_gates = jnp.zeros((row_total,), jnp.float32)
    (grad_rows, gate_rows), (up_grad, down_grad) = lax.scan(one_expert, (start_rows, start_gates), (slot_table, w_up, w_down))
    token_grad = grad_rows.reshape(token_total, top_count, -1).sum(axis=1).astype(jnp.bfloat16)
    gate_grad = gate_rows.reshape(token_total, top_count).astype(jnp.bfloat16)
    return token_grad, gate_grad, up_grad, down_grad
```

```python
import functools
import math

import jax
import jax.numpy as jnp
from jax import lax
from jax.experimental import pallas as pl
from jax.experimental.pallas import tpu as pltpu
from jax.sharding import PartitionSpec as P

GATE_DEN = 256
LANES = 128
BF16 = jnp.bfloat16
F32 = jnp.float32
MESH = pl.DeviceIdType.MESH


def dot(a, b, dims=((1,), (0,))):
    return lax.dot_general(a, b, (dims, ((), ())), preferred_element_type=F32)


def swap_matrix(fold, cap):
    side = fold * fold * cap
    row = lax.broadcasted_iota(jnp.int32, (side, LANES), 0).astype(F32)
    a = jnp.floor((row + 0.5) * (1.0 / (fold * cap)))
    rest = row - a * (fold * cap)
    b = jnp.floor((rest + 0.5) * (1.0 / cap))
    s = rest - b * cap
    source = (b * (fold * cap) + a * cap + s).astype(jnp.int32)
    lane = lax.broadcasted_iota(jnp.int32, (side, LANES), 1)
    parts = []
    for start in range(0, side, LANES):
        parts.append(jnp.where(source == lane + start, 1.0, 0.0).astype(BF16))
    return jnp.concatenate(parts, axis=1)


def slot_one_hot(routes_row, cap, slots):
    count = routes_row.shape[1]
    along = jnp.broadcast_to(routes_row.astype(F32), (count, count))
    down = along.T
    i = lax.broadcasted_iota(jnp.int32, (count, count), 0)
    j = lax.broadcasted_iota(jnp.int32, (count, count), 1)
    rank = jnp.sum(jnp.where((along == down) & (i < j), 1.0, 0.0), axis=0, keepdims=True)
    slot = (routes_row.astype(F32) * cap + rank).astype(jnp.int32)
    number = lax.broadcasted_iota(jnp.int32, (slots, count), 0)
    return jnp.where(number == slot, 1.0, 0.0).astype(BF16)


def spread_matrix(devices, cap, pad):
    rows, columns = devices * pad, devices * cap
    row = lax.broadcasted_iota(jnp.int32, (rows, columns), 0).astype(F32)
    lane = lax.broadcasted_iota(jnp.int32, (rows, columns), 1).astype(F32)
    d = jnp.floor((row + 0.5) * (1.0 / pad))
    s = row - d * pad
    return jnp.where((s < cap) & (d * cap + s == lane), 1.0, 0.0).astype(BF16)


def prepare_kernel(fold, cap, tokens, upstream, routes, shares, send):
    devices, block, width = send.shape
    chunk = width // 2
    count, features = tokens.shape
    gate = jnp.broadcast_to(shares[...].astype(F32) * (1.0 / GATE_DEN), (count, count)).T
    one_hot = slot_one_hot(routes[...], cap, devices * cap)
    swap = swap_matrix(fold, cap)
    scaled = jnp.concatenate(
        [
            (upstream[:, at : at + count].astype(F32) * gate).astype(BF16)
            for at in range(0, features, count)
        ],
        axis=1,
    )
    sent_tokens = dot(one_hot, tokens[...]).astype(BF16)
    sent_scaled = dot(one_hot, scaled).astype(BF16)
    for group in range(devices // fold):
        rows = slice(group * block, (group + 1) * block)
        for half, rows_of in enumerate((sent_tokens, sent_scaled)):
            stacked = jnp.concatenate(
                [rows_of[rows, c * chunk : (c + 1) * chunk] for c in range(fold)], axis=0
            )
            folded = dot(swap, stacked).astype(BF16)
            send[group * fold : (group + 1) * fold, :, half * chunk : (half + 1) * chunk] = (
                folded.reshape(fold, block, chunk)
            )


def exchange_kernel(devices, arrays, *refs):
    sources, targets = refs[:arrays], refs[arrays : 2 * arrays]
    send_sem, recv_sem, own_sem = refs[2 * arrays :]
    me = lax.axis_index("expert")
    barrier = pltpu.get_barrier_semaphore()

    def greet(step, carry):
        pl.semaphore_signal(
            barrier, inc=1, device_id={"expert": lax.rem(me + step, devices)}, device_id_type=MESH
        )
        return carry

    lax.fori_loop(1, devices, greet, 0)
    pl.semaphore_wait(barrier, devices - 1)

    def remote(step, k):
        to = lax.rem(me + step, devices)
        return pltpu.make_async_remote_copy(
            src_ref=sources[k].at[to],
            dst_ref=targets[k].at[me],
            send_sem=send_sem.at[k, step],
            recv_sem=recv_sem.at[k, step],
            device_id={"expert": to},
            device_id_type=MESH,
        )

    def arrival(step, k):
        came = lax.rem(me + devices - step, devices)
        return pltpu.make_async_remote_copy(
            src_ref=sources[k].at[came],
            dst_ref=targets[k].at[came],
            send_sem=send_sem.at[k, step],
            recv_sem=recv_sem.at[k, step],
            device_id={"expert": came},
            device_id_type=MESH,
        )

    def start(step, carry):
        for k in range(arrays):
            remote(step, k).start()
        return carry

    def finish(step, carry):
        for k in range(arrays):
            remote(step, k).wait_send()
            arrival(step, k).wait_recv()
        return carry

    lax.fori_loop(1, devices, start, 0)
    for k in range(arrays):
        own = pltpu.make_async_copy(sources[k].at[me], targets[k].at[me], own_sem.at[k])
        own.start()
        own.wait()
    lax.fori_loop(1, devices, finish, 0)


def exchange(collective_id, *arrays):
    devices = arrays[0].shape[0]
    count = len(arrays)
    return pl.pallas_call(
        functools.partial(exchange_kernel, devices, count),
        out_shape=[jax.ShapeDtypeStruct(a.shape, a.dtype) for a in arrays],
        in_specs=[pl.BlockSpec(memory_space=pl.ANY)] * count,
        out_specs=[pl.BlockSpec(memory_space=pl.ANY)] * count,
        scratch_shapes=[
            pltpu.SemaphoreType.DMA((count, devices)),
            pltpu.SemaphoreType.DMA((count, devices)),
            pltpu.SemaphoreType.DMA((count,)),
        ],
        compiler_params=pltpu.CompilerParams(
            collective_id=collective_id, has_side_effects=True, vmem_limit_bytes=1 << 20
        ),
    )(*arrays)


def unfold(swap, blocks, fold, first, chunk):
    part = blocks[:, :, first : first + chunk]
    return dot(swap, part.reshape(part.shape[0] * part.shape[1], chunk)).astype(BF16)


def expert_kernel(fold, cap, got, w_up, w_down, tokens, scaled, hidden_out, pre_grad_out, back, back_q):
    devices, block, width = got.shape
    chunk = width // 2
    pad = back_q.shape[1]
    swap = swap_matrix(fold, cap)
    for group in range(devices // fold):
        blocks = got[group * fold : (group + 1) * fold]
        for half, out in enumerate((tokens, scaled)):
            rows = unfold(swap, blocks, fold, half * chunk, chunk)
            for c in range(fold):
                out[group * block : (group + 1) * block, c * chunk : (c + 1) * chunk] = rows[
                    c * block : (c + 1) * block
                ]
    pre = dot(tokens[...], w_up[0])
    cotangent = dot(scaled[...], w_down[0])
    sigmoid = jax.nn.sigmoid(pre)
    hidden = (pre * sigmoid).astype(BF16)
    pre_grad = (cotangent * sigmoid * (1.0 + pre * (1.0 - sigmoid))).astype(BF16)
    hidden_out[...] = hidden
    pre_grad_out[...] = pre_grad
    gate_sum = jnp.sum(hidden.astype(F32) * cotangent, axis=1, keepdims=True)
    gate_rows = jnp.broadcast_to(gate_sum, (devices * cap, LANES)).astype(BF16)
    back_q[...] = (
        dot(spread_matrix(devices, cap, pad), gate_rows).astype(BF16).reshape(devices, pad, LANES)
    )
    row_grad = dot(pre_grad, w_up[0], ((1,), (1,))).astype(BF16)
    for group in range(devices // fold):
        rows = slice(group * block, (group + 1) * block)
        stacked = jnp.concatenate(
            [row_grad[rows, c * chunk : (c + 1) * chunk] for c in range(fold)], axis=0
        )
        back[group * fold : (group + 1) * fold] = (
            dot(swap, stacked).astype(BF16).reshape(fold, block, chunk)
        )


def return_kernel(fold, cap, back, back_q, routes, shares, token_grad, gate_grad, rows_ref):
    devices, block, chunk = back.shape
    pad = back_q.shape[1]
    swap = swap_matrix(fold, cap)
    one_hot = slot_one_hot(routes[...], cap, devices * cap)
    for group in range(devices // fold):
        rows = unfold(swap, back[group * fold : (group + 1) * fold], fold, 0, chunk)
        for c in range(fold):
            rows_ref[group * block : (group + 1) * block, c * chunk : (c + 1) * chunk] = rows[
                c * block : (c + 1) * block
            ]
    token_grad[...] = dot(one_hot, rows_ref[...], ((0,), (0,))).astype(BF16)
    spread = spread_matrix(devices, cap, pad)
    sums = dot(spread, back_q[...].reshape(devices * pad, LANES), ((0,), (0,))).astype(BF16)
    per_token = dot(sums, one_hot, ((0,), (0,)))[0:1]
    gate_grad[...] = (per_token / (shares[...].astype(F32) * (1.0 / GATE_DEN))).astype(BF16)


def weight_kernel(tokens, scaled, hidden, pre_grad, up_grad, down_grad):
    up = dot(tokens[...], pre_grad[...], ((0,), (0,))).astype(BF16)
    down = dot(scaled[...], hidden[...], ((0,), (0,))).astype(BF16)
    up_grad[...] = up.astype(up_grad.dtype)[None]
    down_grad[...] = down.astype(down_grad.dtype)[None]


def per_device(tokens, upstream, w_up, w_down, routes, gate_share):
    count, features = tokens.shape
    units = w_up.shape[2]
    devices = lax.axis_size("expert")
    groups = lax.axis_size("dp")
    cap = (3 * count + 2 * devices - 1) // (2 * devices)
    fold = 16 // math.gcd(16, cap)
    block, chunk = fold * cap, features // fold
    slots = devices * cap
    routes_row, shares_row = routes.reshape(1, count), gate_share.reshape(1, count)
    roomy = pltpu.CompilerParams(vmem_limit_bytes=48 << 20)
    send = pl.pallas_call(
        functools.partial(prepare_kernel, fold, cap),
        out_shape=jax.ShapeDtypeStruct((devices, block, 2 * chunk), BF16),
        compiler_params=roomy,
    )(tokens, upstream, routes_row, shares_row)
    (got,) = exchange(1, send)
    got_tokens, got_scaled, hidden, pre_grad, back, back_q = pl.pallas_call(
        functools.partial(expert_kernel, fold, cap),
        out_shape=[
            jax.ShapeDtypeStruct((slots, features), BF16),
            jax.ShapeDtypeStruct((slots, features), BF16),
            jax.ShapeDtypeStruct((slots, units), BF16),
            jax.ShapeDtypeStruct((slots, units), BF16),
            jax.ShapeDtypeStruct((devices, block, chunk), BF16),
            jax.ShapeDtypeStruct((devices, 16, LANES), BF16),
        ],
        compiler_params=roomy,
    )(got, w_up, w_down)
    back, back_q = exchange(2, back, back_q)
    token_grad, gate_grad = pl.pallas_call(
        functools.partial(return_kernel, fold, cap),
        out_shape=[
            jax.ShapeDtypeStruct((count, features), BF16),
            jax.ShapeDtypeStruct((1, count), BF16),
        ],
        scratch_shapes=[pltpu.VMEM((slots, features), BF16)],
        compiler_params=roomy,
    )(back, back_q, routes_row, shares_row)
    tile = 256
    kind = F32 if groups == 1 else BF16
    up_grad, down_grad = pl.pallas_call(
        weight_kernel,
        grid=(features // tile,),
        in_specs=[
            pl.BlockSpec((slots, tile), lambda i: (0, i)),
            pl.BlockSpec((slots, tile), lambda i: (0, i)),
            pl.BlockSpec((slots, units), lambda i: (0, 0)),
            pl.BlockSpec((slots, units), lambda i: (0, 0)),
        ],
        out_specs=[pl.BlockSpec((1, tile, units), lambda i: (0, i, 0))] * 2,
        out_shape=[jax.ShapeDtypeStruct((1, features, units), kind)] * 2,
        compiler_params=roomy,
    )(got_tokens, got_scaled, hidden, pre_grad)
    if groups > 1:
        up_grad, down_grad = (
            lax.psum_scatter(g, "dp", scatter_dimension=1, tiled=True).astype(F32)
            for g in (up_grad, down_grad)
        )
    return token_grad, gate_grad.reshape(count, 1), up_grad, down_grad


def solution(mesh):
    rows, experts = P(("dp", "expert"), None), P("expert", None, None)
    return jax.shard_map(
        per_device,
        mesh=mesh,
        in_specs=(rows, rows, experts, experts, rows, rows),
        out_specs=(rows, rows, P("expert", "dp", None), P("expert", "dp", None)),
        check_vma=False,
    )
```

```python
import functools
import math

import jax
import jax.numpy as jnp
from jax import lax
from jax.experimental import pallas as pl
from jax.experimental.pallas import tpu as pltpu
from jax.sharding import PartitionSpec as P

GATE_DEN = 256
LANES = 128
BF16 = jnp.bfloat16
F32 = jnp.float32
MESH = pl.DeviceIdType.MESH


def dot(a, b, dims=((1,), (0,))):
    return lax.dot_general(a, b, (dims, ((), ())), preferred_element_type=F32)


def swap_matrix(fold, cap):
    side = fold * fold * cap
    row = lax.broadcasted_iota(jnp.int32, (side, LANES), 0).astype(F32)
    a = jnp.floor((row + 0.5) * (1.0 / (fold * cap)))
    rest = row - a * (fold * cap)
    b = jnp.floor((rest + 0.5) * (1.0 / cap))
    s = rest - b * cap
    source = (b * (fold * cap) + a * cap + s).astype(jnp.int32)
    lane = lax.broadcasted_iota(jnp.int32, (side, LANES), 1)
    parts = []
    for start in range(0, side, LANES):
        parts.append(jnp.where(source == lane + start, 1.0, 0.0).astype(BF16))
    return jnp.concatenate(parts, axis=1)


def slot_one_hot(routes_row, cap, slots):
    count = routes_row.shape[1]
    along = jnp.broadcast_to(routes_row.astype(F32), (count, count))
    down = along.T
    i = lax.broadcasted_iota(jnp.int32, (count, count), 0)
    j = lax.broadcasted_iota(jnp.int32, (count, count), 1)
    rank = jnp.sum(jnp.where((along == down) & (i < j), 1.0, 0.0), axis=0, keepdims=True)
    slot = (routes_row.astype(F32) * cap + rank).astype(jnp.int32)
    number = lax.broadcasted_iota(jnp.int32, (slots, count), 0)
    return jnp.where(number == slot, 1.0, 0.0).astype(BF16)


def pick_matrices(devices, cap):
    slots = devices * cap
    d = lax.broadcasted_iota(jnp.int32, (devices, slots), 0).astype(F32)
    slot = lax.broadcasted_iota(jnp.int32, (devices, slots), 1).astype(F32)
    owner = jnp.where(jnp.floor((slot + 0.5) * (1.0 / cap)) == d, 1.0, 0.0)
    slot = lax.broadcasted_iota(jnp.int32, (slots, LANES), 0).astype(F32)
    lane = lax.broadcasted_iota(jnp.int32, (slots, LANES), 1).astype(F32)
    rank = slot - jnp.floor((slot + 0.5) * (1.0 / cap)) * cap
    return owner, jnp.where(rank == lane, 1.0, 0.0)


def fold_rows(swap, rows_of, out, fold):
    devices, block, chunk = out.shape
    for group in range(devices // fold):
        rows = slice(group * block, (group + 1) * block)
        stacked = jnp.concatenate(
            [rows_of[rows, c * chunk : (c + 1) * chunk] for c in range(fold)], axis=0
        )
        out[group * fold : (group + 1) * fold] = (
            dot(swap, stacked).astype(BF16).reshape(fold, block, chunk)
        )


def unfold_rows(swap, blocks, out, fold):
    devices, block, chunk = blocks.shape
    for group in range(devices // fold):
        part = blocks[group * fold : (group + 1) * fold]
        rows = dot(swap, part.reshape(fold * block, chunk)).astype(BF16)
        for c in range(fold):
            out[group * block : (group + 1) * block, c * chunk : (c + 1) * chunk] = rows[
                c * block : (c + 1) * block
            ]


def layer_kernel(
    fold,
    cap,
    tokens,
    upstream,
    routes,
    shares,
    w_up_hbm,
    w_down_hbm,
    tokens_t,
    scaled_t,
    hidden_out,
    pre_grad_out,
    token_grad,
    gate_grad,
    w_up,
    w_down,
    send_tokens,
    send_scaled,
    got_tokens,
    got_scaled,
    send_back,
    got_back,
    send_sums,
    got_sums,
    rows_ref,
    send_sem,
    recv_sem,
    own_sem,
    weight_sem,
):
    devices, block, chunk = send_tokens.shape
    half = devices // 2
    count, features = tokens.shape
    slots = devices * cap
    me = lax.axis_index("expert")
    place = lax.rem(me, half)
    near = me - place
    far = half - near
    channels = (
        (send_tokens, got_tokens),
        (send_scaled, got_scaled),
        (send_back, got_back),
        (send_sums, got_sums),
    )

    up_copy = pltpu.make_async_copy(w_up_hbm.at[0], w_up, weight_sem.at[0])
    down_copy = pltpu.make_async_copy(w_down_hbm.at[0], w_down, weight_sem.at[1])
    up_copy.start()
    down_copy.start()

    barrier = pltpu.get_barrier_semaphore()

    def greet(step, carry):
        pl.semaphore_signal(
            barrier, inc=1, device_id={"expert": lax.rem(me + step, devices)}, device_id_type=MESH
        )
        return carry

    lax.fori_loop(1, devices, greet, 0)

    def copy(k, base, first, step, peer):
        source, target = channels[k]
        return pltpu.make_async_remote_copy(
            src_ref=source.at[peer],
            dst_ref=target.at[me],
            send_sem=send_sem.at[k, first + step],
            recv_sem=recv_sem.at[k, first + step],
            device_id={"expert": peer},
            device_id_type=MESH,
        )

    def push(k, across, step):
        base, first = (far, 0) if across else (near, half)
        peer = base + lax.rem(place + step, half)
        copy(k, base, first, step, peer).start()

    def send_all(k):
        def across(step, carry):
            push(k, True, step)
            return carry

        def within(step, carry):
            push(k, False, step)
            return carry

        lax.fori_loop(0, half, across, 0)
        lax.fori_loop(1, half, within, 0)
        source, target = channels[k]
        pltpu.make_async_copy(source.at[me], target.at[me], own_sem.at[k]).start()

    def drain(k):
        source, target = channels[k]

        def one(first, base, step):
            peer = base + lax.rem(place + step, half)
            copy(k, base, first, step, peer).wait_send()
            came = base + lax.rem(place + half - step, half)
            pltpu.make_async_remote_copy(
                src_ref=source.at[came],
                dst_ref=target.at[came],
                send_sem=send_sem.at[k, first + step],
                recv_sem=recv_sem.at[k, first + step],
                device_id={"expert": came},
                device_id_type=MESH,
            ).wait_recv()

        def across(step, carry):
            one(0, far, step)
            return carry

        def within(step, carry):
            one(half, near, step)
            return carry

        lax.fori_loop(0, half, across, 0)
        lax.fori_loop(1, half, within, 0)
        pltpu.make_async_copy(source.at[me], target.at[me], own_sem.at[k]).wait()

    swap = swap_matrix(fold, cap)
    one_hot = slot_one_hot(routes[...], cap, slots)
    fold_rows(swap, dot(one_hot, tokens[...]).astype(BF16), send_tokens, fold)
    pl.semaphore_wait(barrier, devices - 1)
    send_all(0)
    gate_row = shares[...].astype(F32) * (1.0 / GATE_DEN)
    gate = jnp.broadcast_to(gate_row, (count, count)).T
    scaled = jnp.concatenate(
        [
            (upstream[:, at : at + count].astype(F32) * gate).astype(BF16)
            for at in range(0, features, count)
        ],
        axis=1,
    )
    fold_rows(swap, dot(one_hot, scaled).astype(BF16), send_scaled, fold)
    send_all(1)

    owner, rank = pick_matrices(devices, cap)
    up_copy.wait()
    drain(0)
    unfold_rows(swap, got_tokens, rows_ref, fold)
    pre = dot(rows_ref[...], w_up[...])
    sigmoid = jax.nn.sigmoid(pre)
    hidden = (pre * sigmoid).astype(BF16)
    slope = sigmoid * (1.0 + pre * (1.0 - sigmoid))
    hidden_out[...] = hidden
    tokens_t[...] = rows_ref[...].T

    down_copy.wait()
    drain(1)
    unfold_rows(swap, got_scaled, rows_ref, fold)
    cotangent = dot(rows_ref[...], w_down[...])
    pre_grad = (cotangent * slope).astype(BF16)
    row_grad = dot(pre_grad, w_up[...], ((1,), (1,))).astype(BF16)
    fold_rows(swap, row_grad, send_back, fold)
    send_all(2)
    sums = jnp.sum(hidden.astype(F32) * cotangent, axis=1, keepdims=True).astype(BF16).astype(F32)
    send_sums[...] = dot(owner.astype(BF16), (sums * rank).astype(BF16)).reshape(devices, 1, LANES)
    send_all(3)
    pre_grad_out[...] = pre_grad
    scaled_t[...] = rows_ref[...].T

    drain(3)
    picked = dot(owner.astype(BF16), got_sums[...].reshape(devices, LANES).astype(BF16), ((0,), (0,)))
    picked = jnp.sum(picked * rank, axis=1, keepdims=True)
    per_token = jnp.sum(picked * one_hot.astype(F32), axis=0, keepdims=True)
    gate_grad[...] = (per_token / gate_row).astype(BF16)
    drain(2)
    unfold_rows(swap, got_back, rows_ref, fold)
    token_grad[...] = dot(one_hot, rows_ref[...], ((0,), (0,))).astype(BF16)


def weight_kernel(tokens_t, scaled_t, hidden, pre_grad, up_grad, down_grad):
    up = dot(tokens_t[...], pre_grad[...]).astype(BF16)
    down = dot(scaled_t[...], hidden[...]).astype(BF16)
    up_grad[...] = up.astype(up_grad.dtype)[None]
    down_grad[...] = down.astype(down_grad.dtype)[None]


def per_device(tokens, upstream, w_up, w_down, routes, gate_share):
    count, features = tokens.shape
    units = w_up.shape[2]
    devices = lax.axis_size("expert")
    groups = lax.axis_size("dp")
    cap = (3 * count + 2 * devices - 1) // (2 * devices)
    fold = 16 // math.gcd(16, cap)
    block, chunk = fold * cap, features // fold
    slots = devices * cap
    routes_row, shares_row = routes.reshape(1, count), gate_share.reshape(1, count)
    roomy = pltpu.CompilerParams(vmem_limit_bytes=48 << 20)
    rows = jax.ShapeDtypeStruct((features, slots), BF16)
    units_of = jax.ShapeDtypeStruct((slots, units), BF16)
    whole, outside = pl.BlockSpec(memory_space=pltpu.VMEM), pl.BlockSpec(memory_space=pl.ANY)
    buffer = pltpu.VMEM((devices, block, chunk), BF16)
    sums = pltpu.VMEM((devices, 1, LANES), F32)
    tokens_t, scaled_t, hidden, pre_grad, token_grad, gate_grad = pl.pallas_call(
        functools.partial(layer_kernel, fold, cap),
        in_specs=[whole] * 4 + [outside] * 2,
        out_specs=[whole] * 6,
        out_shape=[
            rows,
            rows,
            units_of,
            units_of,
            jax.ShapeDtypeStruct((count, features), BF16),
            jax.ShapeDtypeStruct((1, count), BF16),
        ],
        scratch_shapes=[
            pltpu.VMEM((features, units), BF16),
            pltpu.VMEM((features, units), BF16),
            *([buffer] * 6),
            sums,
            sums,
            pltpu.VMEM((slots, features), BF16),
            pltpu.SemaphoreType.DMA((4, devices)),
            pltpu.SemaphoreType.DMA((4, devices)),
            pltpu.SemaphoreType.DMA((4,)),
            pltpu.SemaphoreType.DMA((2,)),
        ],
        compiler_params=pltpu.CompilerParams(
            collective_id=1, has_side_effects=True, vmem_limit_bytes=48 << 20
        ),
    )(tokens, upstream, routes_row, shares_row, w_up, w_down)
    tile = 256
    kind = F32 if groups == 1 else BF16
    up_grad, down_grad = pl.pallas_call(
        weight_kernel,
        grid=(features // tile,),
        in_specs=[
            pl.BlockSpec((tile, slots), lambda i: (i, 0)),
            pl.BlockSpec((tile, slots), lambda i: (i, 0)),
            pl.BlockSpec((slots, units), lambda i: (0, 0)),
            pl.BlockSpec((slots, units), lambda i: (0, 0)),
        ],
        out_specs=[pl.BlockSpec((1, tile, units), lambda i: (0, i, 0))] * 2,
        out_shape=[jax.ShapeDtypeStruct((1, features, units), kind)] * 2,
        compiler_params=roomy,
    )(tokens_t, scaled_t, hidden, pre_grad)
    if groups > 1:
        up_grad, down_grad = (
            lax.psum_scatter(g, "dp", scatter_dimension=1, tiled=True).astype(F32)
            for g in (up_grad, down_grad)
        )
    return token_grad, gate_grad.reshape(count, 1), up_grad, down_grad


def solution(mesh):
    rows, experts = P(("dp", "expert"), None), P("expert", None, None)
    return jax.shard_map(
        per_device,
        mesh=mesh,
        in_specs=(rows, rows, experts, experts, rows, rows),
        out_specs=(rows, rows, P("expert", "dp", None), P("expert", "dp", None)),
        check_vma=False,
    )
```

```python
import functools
import math

import jax
import jax.numpy as jnp
from jax import lax
from jax.experimental import pallas as pl
from jax.experimental.pallas import tpu as pltpu
from jax.sharding import PartitionSpec as P

GATE_DEN = 256
LANES = 128
BF16 = jnp.bfloat16
F32 = jnp.float32
MESH = pl.DeviceIdType.MESH


def dot(a, b, dims=((1,), (0,))):
    return lax.dot_general(a, b, (dims, ((), ())), preferred_element_type=F32)


def swap_matrix(fold, cap):
    side = fold * fold * cap
    row = lax.broadcasted_iota(jnp.int32, (side, LANES), 0).astype(F32)
    a = jnp.floor((row + 0.5) * (1.0 / (fold * cap)))
    rest = row - a * (fold * cap)
    b = jnp.floor((rest + 0.5) * (1.0 / cap))
    s = rest - b * cap
    source = (b * (fold * cap) + a * cap + s).astype(jnp.int32)
    lane = lax.broadcasted_iota(jnp.int32, (side, LANES), 1)
    parts = []
    for start in range(0, side, LANES):
        parts.append(jnp.where(source == lane + start, 1.0, 0.0).astype(BF16))
    return jnp.concatenate(parts, axis=1)


def slot_one_hot(routes_row, cap, slots):
    count = routes_row.shape[1]
    along = jnp.broadcast_to(routes_row.astype(F32), (count, count))
    down = along.T
    i = lax.broadcasted_iota(jnp.int32, (count, count), 0)
    j = lax.broadcasted_iota(jnp.int32, (count, count), 1)
    rank = jnp.sum(jnp.where((along == down) & (i < j), 1.0, 0.0), axis=0, keepdims=True)
    slot = (routes_row.astype(F32) * cap + rank).astype(jnp.int32)
    number = lax.broadcasted_iota(jnp.int32, (slots, count), 0)
    return jnp.where(number == slot, 1.0, 0.0).astype(BF16)


def pick_matrices(devices, cap):
    slots = devices * cap
    d = lax.broadcasted_iota(jnp.int32, (devices, slots), 0).astype(F32)
    slot = lax.broadcasted_iota(jnp.int32, (devices, slots), 1).astype(F32)
    owner = jnp.where(jnp.floor((slot + 0.5) * (1.0 / cap)) == d, 1.0, 0.0)
    slot = lax.broadcasted_iota(jnp.int32, (slots, LANES), 0).astype(F32)
    lane = lax.broadcasted_iota(jnp.int32, (slots, LANES), 1).astype(F32)
    rank = slot - jnp.floor((slot + 0.5) * (1.0 / cap)) * cap
    return owner, jnp.where(rank == lane, 1.0, 0.0)


def fold_group(swap, rows, fold):
    block, features = rows.shape
    chunk = features // fold
    stacked = jnp.concatenate([rows[:, c * chunk : (c + 1) * chunk] for c in range(fold)], axis=0)
    return dot(swap, stacked).astype(BF16).reshape(fold, block, chunk)


def unfold_group(swap, part):
    fold, block, chunk = part.shape
    rows = dot(swap, part.reshape(fold * block, chunk)).astype(BF16)
    return jnp.concatenate([rows[c * block : (c + 1) * block] for c in range(fold)], axis=1)


def layer_kernel(
    fold,
    cap,
    tokens_hbm,
    upstream_hbm,
    routes_hbm,
    shares_hbm,
    w_up_hbm,
    w_down_hbm,
    up_grad,
    down_grad,
    token_grad,
    gate_grad,
    tokens,
    upstream,
    routes,
    shares,
    w_up,
    w_down,
    w_up_t,
    send_tokens,
    send_scaled,
    got_tokens,
    got_scaled,
    send_back,
    got_back,
    send_sums,
    got_sums,
    token_rows,
    scaled_rows,
    hidden,
    slope,
    pre_grad,
    sums,
    send_sem,
    recv_sem,
    own_sem,
    load_sem,
):
    devices, block, chunk = send_tokens.shape
    count, features = tokens.shape
    slots = devices * cap
    groups = devices // fold
    side = groups // 2
    me = lax.axis_index("expert")
    place = lax.rem(me, fold)
    mine = lax.div(me, fold)
    lane = lax.rem(mine, side)
    near = mine - lane
    far = side - near
    channels = (
        (send_tokens, got_tokens),
        (send_scaled, got_scaled),
        (send_back, got_back),
        (send_sums, got_sums),
    )
    loads = [
        pltpu.make_async_copy(source, target, load_sem.at[number])
        for number, (source, target) in enumerate(
            (
                (routes_hbm, routes),
                (tokens_hbm, tokens),
                (shares_hbm, shares),
                (upstream_hbm, upstream),
                (w_up_hbm.at[0], w_up),
                (w_down_hbm.at[0], w_down),
            )
        )
    ]
    for load in loads:
        load.start()

    barrier = pltpu.get_barrier_semaphore()

    def greet(step, carry):
        pl.semaphore_signal(
            barrier, inc=1, device_id={"expert": lax.rem(me + step, devices)}, device_id_type=MESH
        )
        return carry

    lax.fori_loop(1, devices, greet, 0)

    def base_of(turn):
        return far + lax.div(turn, side) * (near - far)

    def shift_of(turn):
        return lax.rem(turn + lax.div(turn, side), side)

    def target_group(turn):
        return base_of(turn) + lax.rem(lane + shift_of(turn), side)

    def source_group(turn):
        return base_of(turn) + lax.rem(lane + side - shift_of(turn), side)

    def first_step(turn):
        return lax.div(turn, groups - 1)

    def push(k, turn, step):
        source, target = channels[k]
        peer = target_group(turn) * fold + lax.rem(place + step, fold)
        return pltpu.make_async_remote_copy(
            src_ref=source.at[peer],
            dst_ref=target.at[me],
            send_sem=send_sem.at[k, turn * fold + step],
            recv_sem=recv_sem.at[k, turn * fold + step],
            device_id={"expert": peer},
            device_id_type=MESH,
        )

    def arrival(k, turn, step):
        source, target = channels[k]
        came = source_group(turn) * fold + lax.rem(place + fold - step, fold)
        return pltpu.make_async_remote_copy(
            src_ref=source.at[came],
            dst_ref=target.at[came],
            send_sem=send_sem.at[k, turn * fold + step],
            recv_sem=recv_sem.at[k, turn * fold + step],
            device_id={"expert": came},
            device_id_type=MESH,
        )

    def send_turn(k, turn):
        def one(step, carry):
            push(k, turn, step).start()
            return carry

        lax.fori_loop(first_step(turn), fold, one, 0)

    def await_turn(k, turn):
        def one(step, carry):
            arrival(k, turn, step).wait_recv()
            return carry

        lax.fori_loop(first_step(turn), fold, one, 0)

    def every_turn(act, k):
        def one(turn, carry):
            act(k, turn)
            return carry

        lax.fori_loop(0, groups, one, 0)

    def settle(k, turn):
        def one(step, carry):
            push(k, turn, step).wait_send()
            return carry

        lax.fori_loop(first_step(turn), fold, one, 0)

    def own(k):
        source, target = channels[k]
        return pltpu.make_async_copy(source.at[me], target.at[me], own_sem.at[k])

    swap = swap_matrix(fold, cap)
    loads[0].wait()
    one_hot = slot_one_hot(routes[...], cap, slots)
    loads[1].wait()
    routed = dot(one_hot, tokens[...]).astype(BF16)
    for group in range(groups):
        rows = routed[group * block : (group + 1) * block]
        send_tokens[group * fold : (group + 1) * fold] = fold_group(swap, rows, fold)
    pl.semaphore_wait(barrier, devices - 1)
    every_turn(send_turn, 0)
    own(0).start()
    loads[2].wait()
    loads[3].wait()
    gate_row = shares[...].astype(F32) * (1.0 / GATE_DEN)
    gate = jnp.broadcast_to(gate_row, (count, count)).T
    scaled = jnp.concatenate(
        [
            (upstream[:, at : at + count].astype(F32) * gate).astype(BF16)
            for at in range(0, features, count)
        ],
        axis=1,
    )
    routed = dot(one_hot, scaled).astype(BF16)
    for group in range(groups):
        rows = routed[group * block : (group + 1) * block]
        send_scaled[group * fold : (group + 1) * fold] = fold_group(swap, rows, fold)
    every_turn(send_turn, 1)
    own(1).start()

    owner, rank = pick_matrices(devices, cap)
    loads[4].wait()
    loads[5].wait()
    w_up_t[...] = w_up[...].T
    every_turn(await_turn, 0)
    own(0).wait()
    for group in range(groups):
        token_rows[group * block : (group + 1) * block] = unfold_group(
            swap, got_tokens[group * fold : (group + 1) * fold]
        )
    pre = dot(token_rows[...], w_up[...])
    sigmoid = jax.nn.sigmoid(pre)
    hidden[...] = (pre * sigmoid).astype(BF16)
    slope[...] = sigmoid * (1.0 + pre * (1.0 - sigmoid))

    own(1).wait()

    def group_back(turn, carry):
        group = source_group(turn)
        devs = pl.ds(group * fold, fold)
        rows = pl.ds(pl.multiple_of(group * block, 16), block)
        await_turn(1, turn)
        part = unfold_group(swap, got_scaled[devs])
        scaled_rows[rows] = part
        cotangent = dot(part, w_down[...])
        grad = (cotangent * slope[rows]).astype(BF16)
        pre_grad[rows] = grad
        send_back[devs] = fold_group(swap, dot(grad, w_up_t[...]).astype(BF16), fold)
        back_turn(turn)
        total = jnp.sum(hidden[rows].astype(F32) * cotangent, axis=1, keepdims=True)
        sums[rows] = jnp.broadcast_to(total.astype(BF16).astype(F32), (block, LANES))
        return carry

    def back_turn(turn):
        def one(step, carry):
            peer = source_group(turn) * fold + lax.rem(place + fold - step, fold)
            pltpu.make_async_remote_copy(
                src_ref=send_back.at[peer],
                dst_ref=got_back.at[me],
                send_sem=send_sem.at[2, turn * fold + step],
                recv_sem=recv_sem.at[2, turn * fold + step],
                device_id={"expert": peer},
                device_id_type=MESH,
            ).start()
            return carry

        lax.fori_loop(first_step(turn), fold, one, 0)

    lax.fori_loop(0, groups, group_back, 0)
    own(2).start()
    send_sums[...] = dot(owner.astype(BF16), (sums[...] * rank).astype(BF16)).reshape(
        devices, 1, LANES
    )
    every_turn(send_turn, 3)
    own(3).start()

    tile = 256

    def weights(i, carry):
        at = pl.ds(pl.multiple_of(i * tile, tile), tile)
        up_grad[at] = dot(token_rows[:, at], pre_grad[...], ((0,), (0,))).astype(BF16)
        down_grad[at] = dot(scaled_rows[:, at], hidden[...], ((0,), (0,))).astype(BF16)
        return carry

    lax.fori_loop(0, features // tile, weights, 0)

    every_turn(await_turn, 3)
    own(3).wait()
    picked = dot(owner.astype(BF16), got_sums[...].reshape(devices, LANES).astype(BF16), ((0,), (0,)))
    picked = jnp.sum(picked * rank, axis=1, keepdims=True)
    per_token = jnp.sum(picked * one_hot.astype(F32), axis=0, keepdims=True)
    gate_grad[...] = (per_token / gate_row).astype(BF16)
    for k in (0, 1, 2, 3):
        every_turn(settle, k)

    def await_back(turn, carry):
        def one(step, inner):
            peer = target_group(turn) * fold + lax.rem(place + step, fold)
            pltpu.make_async_remote_copy(
                src_ref=send_back.at[peer],
                dst_ref=got_back.at[peer],
                send_sem=send_sem.at[2, turn * fold + step],
                recv_sem=recv_sem.at[2, turn * fold + step],
                device_id={"expert": peer},
                device_id_type=MESH,
            ).wait_recv()
            return inner

        lax.fori_loop(first_step(turn), fold, one, 0)
        return carry

    lax.fori_loop(0, groups, await_back, 0)
    own(2).wait()
    for group in range(groups):
        token_rows[group * block : (group + 1) * block] = unfold_group(
            swap, got_back[group * fold : (group + 1) * fold]
        )
    token_grad[...] = dot(one_hot, token_rows[...], ((0,), (0,))).astype(BF16)


def per_device(tokens, upstream, w_up, w_down, routes, gate_share):
    count, features = tokens.shape
    units = w_up.shape[2]
    devices = lax.axis_size("expert")
    groups = lax.axis_size("dp")
    cap = (3 * count + 2 * devices - 1) // (2 * devices)
    fold = 16 // math.gcd(16, cap)
    block, chunk = fold * cap, features // fold
    slots = devices * cap
    routes_row, shares_row = routes.reshape(1, count), gate_share.reshape(1, count)
    whole = pl.BlockSpec(memory_space=pltpu.VMEM)
    buffer = pltpu.VMEM((devices, block, chunk), BF16)
    sums = pltpu.VMEM((devices, 1, LANES), F32)
    up_grad, down_grad, token_grad, gate_grad = pl.pallas_call(
        functools.partial(layer_kernel, fold, cap),
        in_specs=[pl.BlockSpec(memory_space=pltpu.HBM)] * 6,
        out_specs=[whole] * 4,
        out_shape=[
            jax.ShapeDtypeStruct((features, units), BF16),
            jax.ShapeDtypeStruct((features, units), BF16),
            jax.ShapeDtypeStruct((count, features), BF16),
            jax.ShapeDtypeStruct((1, count), BF16),
        ],
        scratch_shapes=[
            pltpu.VMEM((count, features), BF16),
            pltpu.VMEM((count, features), BF16),
            pltpu.VMEM((1, count), jnp.int32),
            pltpu.VMEM((1, count), jnp.int32),
            pltpu.VMEM((features, units), BF16),
            pltpu.VMEM((features, units), BF16),
            pltpu.VMEM((units, features), BF16),
            *([buffer] * 6),
            sums,
            sums,
            pltpu.VMEM((slots, features), BF16),
            pltpu.VMEM((slots, features), BF16),
            pltpu.VMEM((slots, units), BF16),
            pltpu.VMEM((slots, units), F32),
            pltpu.VMEM((slots, units), BF16),
            pltpu.VMEM((slots, LANES), F32),
            pltpu.SemaphoreType.DMA((4, devices)),
            pltpu.SemaphoreType.DMA((4, devices)),
            pltpu.SemaphoreType.DMA((4,)),
            pltpu.SemaphoreType.DMA((6,)),
        ],
        compiler_params=pltpu.CompilerParams(
            collective_id=1, has_side_effects=True, vmem_limit_bytes=48 << 20
        ),
    )(tokens, upstream, routes_row, shares_row, w_up, w_down)
    up_grad, down_grad = up_grad[None], down_grad[None]
    if groups > 1:
        up_grad, down_grad = (
            lax.psum_scatter(g, "dp", scatter_dimension=1, tiled=True)
            for g in (up_grad, down_grad)
        )
    return token_grad, gate_grad.reshape(count, 1), up_grad.astype(F32), down_grad.astype(F32)


def solution(mesh):
    rows, experts = P(("dp", "expert"), None), P("expert", None, None)
    return jax.shard_map(
        per_device,
        mesh=mesh,
        in_specs=(rows, rows, experts, experts, rows, rows),
        out_specs=(rows, rows, P("expert", "dp", None), P("expert", "dp", None)),
        check_vma=False,
    )
```

```python
import functools
import math

import jax
import jax.numpy as jnp
from jax import lax
from jax.experimental import pallas as pl
from jax.experimental.pallas import tpu as pltpu
from jax.sharding import PartitionSpec as P

GATE_DEN = 256
LANES = 128
BF16 = jnp.bfloat16
F32 = jnp.float32
MESH = pl.DeviceIdType.MESH


def dot(a, b, dims=((1,), (0,))):
    return lax.dot_general(a, b, (dims, ((), ())), preferred_element_type=F32)


def swap_matrix(fold, cap):
    side = fold * fold * cap
    row = lax.broadcasted_iota(jnp.int32, (side, LANES), 0).astype(F32)
    a = jnp.floor((row + 0.5) * (1.0 / (fold * cap)))
    rest = row - a * (fold * cap)
    b = jnp.floor((rest + 0.5) * (1.0 / cap))
    s = rest - b * cap
    source = (b * (fold * cap) + a * cap + s).astype(jnp.int32)
    lane = lax.broadcasted_iota(jnp.int32, (side, LANES), 1)
    parts = []
    for start in range(0, side, LANES):
        parts.append(jnp.where(source == lane + start, 1.0, 0.0).astype(BF16))
    return jnp.concatenate(parts, axis=1)


def slot_one_hot(routes_row, cap, slots):
    count = routes_row.shape[1]
    along = jnp.broadcast_to(routes_row.astype(F32), (count, count))
    down = along.T
    i = lax.broadcasted_iota(jnp.int32, (count, count), 0)
    j = lax.broadcasted_iota(jnp.int32, (count, count), 1)
    rank = jnp.sum(jnp.where((along == down) & (i < j), 1.0, 0.0), axis=0, keepdims=True)
    slot = (routes_row.astype(F32) * cap + rank).astype(jnp.int32)
    number = lax.broadcasted_iota(jnp.int32, (slots, count), 0)
    return jnp.where(number == slot, 1.0, 0.0).astype(BF16)


def pick_matrices(devices, cap):
    slots = devices * cap
    d = lax.broadcasted_iota(jnp.int32, (devices, slots), 0).astype(F32)
    slot = lax.broadcasted_iota(jnp.int32, (devices, slots), 1).astype(F32)
    owner = jnp.where(jnp.floor((slot + 0.5) * (1.0 / cap)) == d, 1.0, 0.0)
    slot = lax.broadcasted_iota(jnp.int32, (slots, LANES), 0).astype(F32)
    lane = lax.broadcasted_iota(jnp.int32, (slots, LANES), 1).astype(F32)
    rank = slot - jnp.floor((slot + 0.5) * (1.0 / cap)) * cap
    return owner, jnp.where(rank == lane, 1.0, 0.0)


def fold_group(swap, rows, fold):
    block, features = rows.shape
    chunk = features // fold
    stacked = jnp.concatenate([rows[:, c * chunk : (c + 1) * chunk] for c in range(fold)], axis=0)
    return dot(swap, stacked).astype(BF16).reshape(fold, block, chunk)


def unfold_group(swap, part):
    fold, block, chunk = part.shape
    rows = dot(swap, part.reshape(fold * block, chunk)).astype(BF16)
    return jnp.concatenate([rows[c * block : (c + 1) * block] for c in range(fold)], axis=1)


def layer_kernel(
    fold,
    cap,
    tokens_hbm,
    upstream_hbm,
    routes_hbm,
    shares_hbm,
    w_up_hbm,
    w_down_hbm,
    token_rows,
    scaled_rows,
    hidden,
    pre_grad,
    token_grad,
    gate_grad,
    tokens,
    upstream,
    routes,
    shares,
    w_up,
    w_down,
    w_up_t,
    send_tokens,
    send_scaled,
    got_tokens,
    got_scaled,
    send_back,
    got_back,
    send_sums,
    got_sums,
    back_rows,
    slope,
    sums,
    send_sem,
    recv_sem,
    own_sem,
    load_sem,
):
    devices, block, chunk = send_tokens.shape
    count, features = tokens.shape
    slots = devices * cap
    groups = devices // fold
    side = groups // 2
    me = lax.axis_index("expert")
    place = lax.rem(me, fold)
    mine = lax.div(me, fold)
    lane = lax.rem(mine, side)
    near = mine - lane
    far = side - near
    channels = (
        (send_tokens, got_tokens),
        (send_scaled, got_scaled),
        (send_back, got_back),
        (send_sums, got_sums),
    )
    loads = [
        pltpu.make_async_copy(source, target, load_sem.at[number])
        for number, (source, target) in enumerate(
            (
                (routes_hbm, routes),
                (tokens_hbm, tokens),
                (shares_hbm, shares),
                (upstream_hbm, upstream),
                (w_up_hbm.at[0], w_up),
                (w_down_hbm.at[0], w_down),
            )
        )
    ]
    for load in loads:
        load.start()

    barrier = pltpu.get_barrier_semaphore()

    def greet(step, carry):
        pl.semaphore_signal(
            barrier, inc=1, device_id={"expert": lax.rem(me + step, devices)}, device_id_type=MESH
        )
        return carry

    lax.fori_loop(1, devices, greet, 0)

    def base_of(turn):
        return far + lax.div(turn, side) * (near - far)

    def shift_of(turn):
        return lax.rem(turn + lax.div(turn, side), side)

    def target_group(turn):
        return base_of(turn) + lax.rem(lane + shift_of(turn), side)

    def source_group(turn):
        return base_of(turn) + lax.rem(lane + side - shift_of(turn), side)

    def first_step(turn):
        return lax.div(turn, groups - 1)

    def push(k, turn, step):
        source, target = channels[k]
        peer = target_group(turn) * fold + lax.rem(place + step, fold)
        return pltpu.make_async_remote_copy(
            src_ref=source.at[peer],
            dst_ref=target.at[me],
            send_sem=send_sem.at[k, turn * fold + step],
            recv_sem=recv_sem.at[k, turn * fold + step],
            device_id={"expert": peer},
            device_id_type=MESH,
        )

    def arrival(k, turn, step):
        source, target = channels[k]
        came = source_group(turn) * fold + lax.rem(place + fold - step, fold)
        return pltpu.make_async_remote_copy(
            src_ref=source.at[came],
            dst_ref=target.at[came],
            send_sem=send_sem.at[k, turn * fold + step],
            recv_sem=recv_sem.at[k, turn * fold + step],
            device_id={"expert": came},
            device_id_type=MESH,
        )

    def send_turn(k, turn):
        def one(step, carry):
            push(k, turn, step).start()
            return carry

        lax.fori_loop(first_step(turn), fold, one, 0)

    def await_turn(k, turn):
        def one(step, carry):
            arrival(k, turn, step).wait_recv()
            return carry

        lax.fori_loop(first_step(turn), fold, one, 0)

    def every_turn(act, k):
        def one(turn, carry):
            act(k, turn)
            return carry

        lax.fori_loop(0, groups, one, 0)

    def settle(k, turn):
        def one(step, carry):
            push(k, turn, step).wait_send()
            return carry

        lax.fori_loop(first_step(turn), fold, one, 0)

    def own(k):
        source, target = channels[k]
        return pltpu.make_async_copy(source.at[me], target.at[me], own_sem.at[k])

    swap = swap_matrix(fold, cap)
    loads[0].wait()
    one_hot = slot_one_hot(routes[...], cap, slots)
    loads[1].wait()
    routed = dot(one_hot, tokens[...]).astype(BF16)
    for group in range(groups):
        rows = routed[group * block : (group + 1) * block]
        send_tokens[group * fold : (group + 1) * fold] = fold_group(swap, rows, fold)
    pl.semaphore_wait(barrier, devices - 1)
    every_turn(send_turn, 0)
    own(0).start()
    loads[2].wait()
    loads[3].wait()
    gate_row = shares[...].astype(F32) * (1.0 / GATE_DEN)
    gate = jnp.broadcast_to(gate_row, (count, count)).T
    scaled = jnp.concatenate(
        [
            (upstream[:, at : at + count].astype(F32) * gate).astype(BF16)
            for at in range(0, features, count)
        ],
        axis=1,
    )
    routed = dot(one_hot, scaled).astype(BF16)
    for group in range(groups):
        rows = routed[group * block : (group + 1) * block]
        send_scaled[group * fold : (group + 1) * fold] = fold_group(swap, rows, fold)
    every_turn(send_turn, 1)
    own(1).start()

    owner, rank = pick_matrices(devices, cap)
    loads[4].wait()
    loads[5].wait()
    w_up_t[...] = w_up[...].T
    every_turn(await_turn, 0)
    own(0).wait()
    for group in range(groups):
        token_rows[group * block : (group + 1) * block] = unfold_group(
            swap, got_tokens[group * fold : (group + 1) * fold]
        )
    pre = dot(token_rows[...], w_up[...])
    sigmoid = jax.nn.sigmoid(pre)
    hidden[...] = (pre * sigmoid).astype(BF16)
    slope[...] = sigmoid * (1.0 + pre * (1.0 - sigmoid))

    own(1).wait()

    def group_back(turn, carry):
        group = source_group(turn)
        devs = pl.ds(group * fold, fold)
        rows = pl.ds(pl.multiple_of(group * block, 16), block)
        await_turn(1, turn)
        part = unfold_group(swap, got_scaled[devs])
        scaled_rows[rows] = part
        cotangent = dot(part, w_down[...])
        grad = (cotangent * slope[rows]).astype(BF16)
        pre_grad[rows] = grad
        send_back[devs] = fold_group(swap, dot(grad, w_up_t[...]).astype(BF16), fold)
        back_turn(turn)
        total = jnp.sum(hidden[rows].astype(F32) * cotangent, axis=1, keepdims=True)
        sums[rows] = jnp.broadcast_to(total.astype(BF16).astype(F32), (block, LANES))
        return carry

    def back_turn(turn):
        def one(step, carry):
            peer = source_group(turn) * fold + lax.rem(place + fold - step, fold)
            pltpu.make_async_remote_copy(
                src_ref=send_back.at[peer],
                dst_ref=got_back.at[me],
                send_sem=send_sem.at[2, turn * fold + step],
                recv_sem=recv_sem.at[2, turn * fold + step],
                device_id={"expert": peer},
                device_id_type=MESH,
            ).start()
            return carry

        lax.fori_loop(first_step(turn), fold, one, 0)

    lax.fori_loop(0, groups, group_back, 0)
    own(2).start()
    send_sums[...] = dot(owner.astype(BF16), (sums[...] * rank).astype(BF16)).reshape(
        devices, 1, LANES
    )
    every_turn(send_turn, 3)
    own(3).start()

    every_turn(await_turn, 3)
    own(3).wait()
    picked = dot(owner.astype(BF16), got_sums[...].reshape(devices, LANES).astype(BF16), ((0,), (0,)))
    picked = jnp.sum(picked * rank, axis=1, keepdims=True)
    per_token = jnp.sum(picked * one_hot.astype(F32), axis=0, keepdims=True)
    gate_grad[...] = (per_token / gate_row).astype(BF16)
    for k in (0, 1, 2, 3):
        every_turn(settle, k)

    def await_back(turn, carry):
        def one(step, inner):
            peer = target_group(turn) * fold + lax.rem(place + step, fold)
            pltpu.make_async_remote_copy(
                src_ref=send_back.at[peer],
                dst_ref=got_back.at[peer],
                send_sem=send_sem.at[2, turn * fold + step],
                recv_sem=recv_sem.at[2, turn * fold + step],
                device_id={"expert": peer},
                device_id_type=MESH,
            ).wait_recv()
            return inner

        lax.fori_loop(first_step(turn), fold, one, 0)
        return carry

    lax.fori_loop(0, groups, await_back, 0)
    own(2).wait()
    for group in range(groups):
        back_rows[group * block : (group + 1) * block] = unfold_group(
            swap, got_back[group * fold : (group + 1) * fold]
        )
    token_grad[...] = dot(one_hot, back_rows[...], ((0,), (0,))).astype(BF16)


def weight_kernel(tokens, scaled, hidden, pre_grad, up_grad, down_grad):
    up = dot(tokens[...], pre_grad[...], ((0,), (0,))).astype(BF16)
    down = dot(scaled[...], hidden[...], ((0,), (0,))).astype(BF16)
    up_grad[...] = up.astype(up_grad.dtype)[None]
    down_grad[...] = down.astype(down_grad.dtype)[None]


def per_device(tokens, upstream, w_up, w_down, routes, gate_share):
    count, features = tokens.shape
    units = w_up.shape[2]
    devices = lax.axis_size("expert")
    groups = lax.axis_size("dp")
    cap = (3 * count + 2 * devices - 1) // (2 * devices)
    fold = 16 // math.gcd(16, cap)
    block, chunk = fold * cap, features // fold
    slots = devices * cap
    routes_row, shares_row = routes.reshape(1, count), gate_share.reshape(1, count)
    whole = pl.BlockSpec(memory_space=pltpu.VMEM)
    buffer = pltpu.VMEM((devices, block, chunk), BF16)
    sums = pltpu.VMEM((devices, 1, LANES), F32)
    got_tokens, got_scaled, hidden, pre_grad, token_grad, gate_grad = pl.pallas_call(
        functools.partial(layer_kernel, fold, cap),
        in_specs=[pl.BlockSpec(memory_space=pltpu.HBM)] * 6,
        out_specs=[whole] * 6,
        out_shape=[
            jax.ShapeDtypeStruct((slots, features), BF16),
            jax.ShapeDtypeStruct((slots, features), BF16),
            jax.ShapeDtypeStruct((slots, units), BF16),
            jax.ShapeDtypeStruct((slots, units), BF16),
            jax.ShapeDtypeStruct((count, features), BF16),
            jax.ShapeDtypeStruct((1, count), BF16),
        ],
        scratch_shapes=[
            pltpu.VMEM((count, features), BF16),
            pltpu.VMEM((count, features), BF16),
            pltpu.VMEM((1, count), jnp.int32),
            pltpu.VMEM((1, count), jnp.int32),
            pltpu.VMEM((features, units), BF16),
            pltpu.VMEM((features, units), BF16),
            pltpu.VMEM((units, features), BF16),
            *([buffer] * 6),
            sums,
            sums,
            pltpu.VMEM((slots, features), BF16),
            pltpu.VMEM((slots, units), F32),
            pltpu.VMEM((slots, LANES), F32),
            pltpu.SemaphoreType.DMA((4, devices)),
            pltpu.SemaphoreType.DMA((4, devices)),
            pltpu.SemaphoreType.DMA((4,)),
            pltpu.SemaphoreType.DMA((6,)),
        ],
        compiler_params=pltpu.CompilerParams(
            collective_id=1, has_side_effects=True, vmem_limit_bytes=127 << 19
        ),
    )(tokens, upstream, routes_row, shares_row, w_up, w_down)
    tile = 256
    kind = F32 if groups == 1 else BF16
    up_grad, down_grad = pl.pallas_call(
        weight_kernel,
        grid=(features // tile,),
        in_specs=[
            pl.BlockSpec((slots, tile), lambda i: (0, i)),
            pl.BlockSpec((slots, tile), lambda i: (0, i)),
            pl.BlockSpec((slots, units), lambda i: (0, 0)),
            pl.BlockSpec((slots, units), lambda i: (0, 0)),
        ],
        out_specs=[pl.BlockSpec((1, tile, units), lambda i: (0, i, 0))] * 2,
        out_shape=[jax.ShapeDtypeStruct((1, features, units), kind)] * 2,
        compiler_params=pltpu.CompilerParams(vmem_limit_bytes=127 << 19),
    )(got_tokens, got_scaled, hidden, pre_grad)
    if groups > 1:
        up_grad, down_grad = (
            lax.psum_scatter(g, "dp", scatter_dimension=1, tiled=True)
            for g in (up_grad, down_grad)
        )
    return token_grad, gate_grad.reshape(count, 1), up_grad.astype(F32), down_grad.astype(F32)


def solution(mesh):
    rows, experts = P(("dp", "expert"), None), P("expert", None, None)
    return jax.shard_map(
        per_device,
        mesh=mesh,
        in_specs=(rows, rows, experts, experts, rows, rows),
        out_specs=(rows, rows, P("expert", "dp", None), P("expert", "dp", None)),
        check_vma=False,
    )
```
